32 devices in a mesh: group: 2 (over x), wide: 16 (over z, y, core).
Axes of the slice: x: 2, y: 2, z: 4, core: 2. Of those that a mesh axis runs over, the one named last changes fastest.
Arguments:
- tokens: bfloat16 [4096, 4096], P(('group', 'wide')), parts along dimension 0, may hold values from -6 to 6
- cotangent: bfloat16 [4096, 4096], P(('group', 'wide')), parts along dimension 0, may hold values from -18 to 18
- expert_ids: int32 [4096, 4], P(('group', 'wide')), parts along dimension 0, may hold values from 0 to 15, all different within a row; in each aligned block of 128 rows (0 to 127, 128 to 255, ...) at most 48 rows name the same one
- gate_codes: int32 [4096, 4], P(('group', 'wide')), parts along dimension 0, may hold values from 1 to 1023
- w_gate: bfloat16 [16, 4096, 768], P('wide'), may hold values from -0.09375 to 0.09375
- w_up: bfloat16 [16, 4096, 768], P('wide'), may hold values from -0.09375 to 0.09375
- w_down: bfloat16 [16, 768, 4096], P('wide'), may hold values from -0.21875 to 0.21875
Outputs:
- moe_out: bfloat16 [4096, 4096], P(('group', 'wide')), parts along dimension 0
- token_grad: bfloat16 [4096, 4096], P(('group', 'wide')), parts along dimension 0
The draws below stay inside these ranges and needn't reach their ends.
There are 2 independent parts, one for each index of `group`. The reference program is written for one: setup_inputs(seed, part) draws one part's arguments, and reference() takes and returns one part's arrays. A program takes and returns all parts, laid end to end along the dimension named above; an argument that names none is the same for every part. Nothing has to cross between parts.
Inputs may be any that keep to these rules, and one draw needn't show every extreme that they name: `expert_ids`: each token names 4 different experts; among the routes of the tokens of one device no expert is named more than 48 times.
All inputs are finite; a program needn't handle non-finite values.
Results may differ from the reference program's by a relative error of at most 0.0064.
Values may be sent and summed in bfloat16 or wider, within the bound.
No kernel may reach another device: no remote copies, remote signals or barrier semaphores. Data moves between devices by JAX's collectives and lax.ppermute only.
A program may use at most 128 MiB of HBM per device.

```python
import math
import jax
import jax.numpy as jnp
import numpy as np
from jax import lax

D = 4096
FF = 768
TOPK = 4
TOK_DEV = 128
EXPERTS = 16
TOKENS = 2048
CAP = 48


def place_ends(result, stream_key, low, top_value):
    longest = result.shape.index(max(result.shape))
    spots = []
    for shift in (0, 1):
        where = [jax.random.randint(jax.random.fold_in(stream_key, axis), (), 0, length) for axis, length in enumerate(result.shape)]
        where[longest] = (where[longest] + shift) % result.shape[longest]
        spots.append(tuple(where))
    return result.at[spots[0]].set(low).at[spots[1]].set(top_value)


def level_of(own_key, dims, cuts, smallest, top_value):
    def one(dim, shards_of):
        heights = jax.random.uniform(jax.random.fold_in(jax.random.fold_in(own_key, 6), dim), (shards_of,), jnp.float32, smallest / len(cuts), top_value / len(cuts))
        return jnp.repeat(jnp.exp(heights), dims[dim] // shards_of).reshape((-1,) + (1,) * (len(dims) - dim - 1))

    factor_of = one(*cuts[0])
    for cut in cuts[1:]:
        factor_of = factor_of * one(*cut)
    return factor_of


def routed_block(key, own, number, rows, amount, top, bound, slope):
    sequence = jax.random.permutation(key, amount)
    crowded, common = shares(amount, rows * top, bound, slope, True), shares(amount, rows * top, bound, slope, False)
    places = jnp.arange(amount)

    def named(sizes, rotation):
        used = int((sizes > 0).sum())
        fixed = max(1, used // 4)
        moved = fixed + (places - fixed + rotation * (used - fixed)) % max(1, amount - fixed)
        return jnp.zeros((amount,), jnp.int32).at[sequence[jnp.where(places < fixed, places, moved)]].set(jnp.asarray(sizes, jnp.int32))

    sizes = jnp.where(number % 4 == 0, named(crowded, number // 4), named(common, number - number // 4 - 1))
    mixed = jax.random.permutation(jax.random.fold_in(own, 3), amount)
    giver, sink = mixed[0:amount // 2 * 2:2], mixed[1:amount // 2 * 2:2]
    slack = jnp.minimum(sizes[giver] - 1, bound - sizes[sink]) // 2
    slack = jnp.where((giver == sequence[0]) | (sink == sequence[0]) | (sizes[sink] == 0), 0, jnp.maximum(slack, 0))
    moved = jax.random.randint(jax.random.fold_in(own, 4), (amount // 2,), 0, 1 << 20) % (slack + 1)
    sizes = sizes.at[giver].add(-moved).at[sink].add(moved)
    items = jnp.searchsorted(jnp.cumsum(sizes), jnp.arange(rows * top), side="right").astype(jnp.int32)
    listing = items.reshape(top, rows).T
    listing = listing[jax.random.permutation(jax.random.fold_in(own, 1), rows)]
    rotation = jax.random.randint(jax.random.fold_in(own, 2), (rows, 1), 0, top)
    return jnp.take_along_axis(listing, (jnp.arange(top)[None, :] + rotation) % top, axis=1)


def shares(number_of, total, limit, lean, full):
    loads = [(1 << 20) // math.isqrt(grade ** lean) + 1 for grade in range(1, number_of + 1)]
    largest = limit if full else min(limit, max(-(-total // number_of), total * loads[0] // sum(loads)))
    least = 1 if total - largest >= number_of - 1 else 0
    given, surplus = [largest] + [least] * (number_of - 1), total - largest - least * (number_of - 1)
    while surplus > 0:
        free = [i for i in range(1, number_of) if given[i] < largest] or [i for i in range(1, number_of) if given[i] < limit]
        pool, remaining = sum([loads[i] for i in free]), surplus
        for i in free:
            extra = min(limit - given[i], max(1, remaining * loads[i] // pool), surplus)
            given[i] = given[i] + extra
            surplus = surplus - extra
    return np.array(given)


def normal_values(stream_key, shape, deviation, limit, split=(), kind=jnp.bfloat16):
    factor_of = level_of(stream_key, shape, split, -0.22, 0.18) if split else 1.0
    drawn = jax.random.normal(stream_key, shape, jnp.float32) * deviation * factor_of
    return jnp.minimum(jnp.maximum(drawn, -limit), limit).astype(kind)


def setup_inputs(seed: int = 0, part: int = 0) -> dict:
    seeds = jax.random.split(jax.random.key(seed), 8)
    part_keys = jax.random.split(jax.random.fold_in(seeds[7], part), 8)
    tokens = normal_values(part_keys[0], (TOKENS, D), 1.0, 6.0, ((0, 16),))
    cotangent = normal_values(part_keys[1], (TOKENS, D), 3.0, 18.0, ((0, 16),))
    expert_ids_keys = jax.random.split(jax.random.fold_in(part_keys[2], 1), TOKENS // TOK_DEV)
    expert_ids_turns = jax.random.permutation(jax.random.fold_in(part_keys[2], 3), TOKENS // TOK_DEV)
    expert_ids = jax.vmap(lambda own, number: routed_block(jax.random.fold_in(part_keys[2], 2), own, number, TOK_DEV, EXPERTS, TOPK, CAP, 2))(expert_ids_keys, expert_ids_turns).reshape((TOKENS, TOPK))
    gate_codes = place_ends(jax.random.randint(part_keys[3], (TOKENS, TOPK), 1, 1024), jax.random.fold_in(part_keys[3], 1), 1, 1023).astype(jnp.int32)
    w_gate = normal_values(seeds[4], (EXPERTS, D, FF), D ** -0.5, 0.09375, ((0, 16),))
    w_up = normal_values(seeds[5], (EXPERTS, D, FF), D ** -0.5, 0.09375, ((0, 16),))
    w_down = normal_values(seeds[6], (EXPERTS, FF, D), FF ** -0.5, 0.21875, ((0, 16),))
    return dict(tokens=tokens, cotangent=cotangent, expert_ids=expert_ids, gate_codes=gate_codes, w_gate=w_gate, w_up=w_up, w_down=w_down)


def expert_pass(inputs_rows, cot_rows, gate_mat, up_mat, down_mat):
    pre_gate = jnp.dot(inputs_rows, gate_mat, preferred_element_type=jnp.float32)
    pre_up = jnp.dot(inputs_rows, up_mat, preferred_element_type=jnp.float32)
    logistic = jax.nn.sigmoid(pre_gate)
    activated = pre_gate * logistic
    hidden = (activated * pre_up).astype(jnp.bfloat16)
    outputs = jnp.dot(hidden, down_mat, preferred_element_type=jnp.float32).astype(jnp.bfloat16)
    hidden_grad = jnp.dot(cot_rows, down_mat.T, preferred_element_type=jnp.float32)
    gate_grad = (hidden_grad * pre_up * logistic * (1.0 + pre_gate * (1.0 - logistic))).astype(jnp.bfloat16)
    up_grad = (hidden_grad * activated).astype(jnp.bfloat16)
    input_grad = (jnp.dot(gate_grad, gate_mat.T, preferred_element_type=jnp.float32)
                  + jnp.dot(up_grad, up_mat.T, preferred_element_type=jnp.float32)).astype(jnp.bfloat16)
    return outputs, input_grad


def reference(tokens, cotangent, expert_ids, gate_codes, w_gate, w_up, w_down):
    gate_values = gate_codes.astype(jnp.float32)
    gate_share = gate_values / jnp.sum(gate_values, axis=1, keepdims=True)
    flat_ids = expert_ids.reshape(-1)
    flat_share = gate_share.reshape(-1)
    slot_total = EXPERTS * CAP

    def per_expert(totals, expert):
        moe_total, grad_total = totals
        matches = flat_ids == expert
        selected = jnp.nonzero(matches, size=slot_total, fill_value=0)[0].astype(jnp.int32)
        valid = jnp.arange(slot_total, dtype=jnp.int32) < jnp.sum(matches.astype(jnp.int32))
        token_index = (selected // TOPK).astype(jnp.int32)
        route_gate = jnp.where(valid, flat_share[selected], 0.0)
        inputs_rows = tokens[token_index]
        cot_rows = (route_gate[:, None] * cotangent[token_index].astype(jnp.float32)).astype(jnp.bfloat16)
        outputs, input_grad = expert_pass(inputs_rows, cot_rows, w_gate[expert], w_up[expert], w_down[expert])
        moe_total = moe_total.at[token_index].add(route_gate[:, None] * outputs.astype(jnp.float32))
        grad_total = grad_total.at[token_index].add(jnp.where(valid[:, None], input_grad.astype(jnp.float32), 0.0))
        return (moe_total, grad_total), None

    zeros = jnp.zeros(tokens.shape, jnp.float32)
    (moe_total, grad_total), _ = lax.scan(per_expert, (zeros, zeros), jnp.arange(EXPERTS, dtype=jnp.int32))
    return moe_total.astype(jnp.bfloat16), grad_total.astype(jnp.bfloat16)
```

```python
import jax
import jax.numpy as jnp
from jax import lax
from jax.sharding import PartitionSpec as P

contract_last = (((1,), (1,)), ((), ()))
contract_first = (((0,), (0,)), ((), ()))
STREAMS = 2


def layout(wide):
    if wide == 16:
        return 4, 2, (0, 1, 3, 2)
    return wide // 2, 1, tuple(range(wide // 2))


def per_device(tokens, cotangent, expert_ids, gate_codes, w_gate, w_up, w_down):
    wide = lax.axis_size("wide")
    rows, width = tokens.shape
    top = expert_ids.shape[1]
    cap = 3 * rows * top // (2 * wide)
    zs, ys, ring = layout(wide)
    me = lax.axis_index("wide")
    core, col, my_z = me % 2, (me // 2) % ys, me // (2 * ys)

    def pairs(move):
        out = []
        for z in range(zs):
            for y in range(ys):
                for c in range(2):
                    tz, ty, tc = move(z, y, c)
                    out.append(((z * ys + y) * 2 + c, (tz * ys + ty) * 2 + tc))
        return out

    place = {z: i for i, z in enumerate(ring)}
    ahead = pairs(lambda z, y, c: (ring[(place[z] + 1) % zs], y, c))
    back = pairs(lambda z, y, c: (ring[(place[z] - 1) % zs], y, c))
    across = pairs(lambda z, y, c: (z, (y + 1) % ys, c))
    twin = pairs(lambda z, y, c: (z, y, 1 - c))

    def permute(value, perm):
        return lax.ppermute(value, "wide", perm)

    codes = lax.all_gather(jnp.concatenate([expert_ids, gate_codes], axis=1), "wide")
    codes = codes.reshape(zs, ys, 2, rows, 2 * top)
    codes = lax.dynamic_index_in_dim(codes, core, 2, keepdims=False)
    order = jnp.array([[ring[(place[z] - r) % zs] for r in range(zs)] for z in range(zs)], jnp.int32)
    codes = codes[order[my_z]]
    mine = lax.dynamic_index_in_dim(codes, col, 1, keepdims=False)
    sides = [mine]
    if ys == 2:
        sides.append(lax.dynamic_index_in_dim(codes, 1 - col, 1, keepdims=False))
    chip = my_z * ys + col
    here = jnp.stack([2 * chip + core, 2 * chip + 1 - core])
    chips = [here]
    if ys == 2:
        there = my_z * ys + 1 - col
        chips.append(jnp.stack([2 * there + core, 2 * there + 1 - core]))

    def table(side, experts):
        ids, gates = side[..., :top], side[..., top:].astype(jnp.float32)
        share = gates / jnp.sum(gates, axis=-1, keepdims=True)
        same = ids[:, None] == experts[None, :, None, None]
        hit = jnp.any(same, axis=-1)
        gate = jnp.sum(jnp.where(same, share[:, None], 0.0), axis=-1)
        spot = jnp.cumsum(hit.astype(jnp.int32), axis=-1) - 1
        pick = hit[:, :, None] & (spot[:, :, None] == jnp.arange(cap)[None, None, :, None])
        slot_gate = jnp.sum(jnp.where(pick, gate[:, :, None], 0.0), axis=-1)
        return pick.astype(jnp.bfloat16), slot_gate

    pick_here, gate_here = table(mine, here)
    picks, gates = [pick_here], [gate_here]
    if ys == 2:
        pick_there, gate_there = table(mine, chips[1])
        picks.append(pick_there)
        gates.append(gate_there)
    pick = jnp.concatenate(picks, axis=1).reshape(zs, -1, rows)
    pick_gate = jnp.concatenate(gates, axis=1).reshape(zs, -1)
    slots = 2 * cap
    expert_gate = [gate_here]
    if ys == 2:
        expert_gate.append(table(sides[1], here)[1])
    expert_gate = jnp.concatenate(expert_gate, axis=0)

    def cut(value):
        step = width // STREAMS
        return [value[:, i * step : (i + 1) * step] for i in range(STREAMS)]

    def dispatch(value, weighted):
        parts = cut(value)
        own, other = [], []
        for r in range(zs):
            chosen = [
                lax.dot_general(pick[r], part, (((1,), (0,)), ((), ())), preferred_element_type=jnp.float32)
                for part in parts
            ]
            if weighted:
                chosen = [pick_gate[r][:, None] * part for part in chosen]
            chosen = jnp.concatenate([part.astype(jnp.bfloat16) for part in chosen], axis=1)
            own.append(chosen[:slots])
            if ys == 2:
                other.append(permute(chosen[slots:], across))
            if r < zs - 1:
                parts = [permute(part, ahead) for part in parts]
        sources = own + other
        return [jnp.concatenate([s[e * cap : (e + 1) * cap] for s in sources], axis=0) for e in range(2)]

    def combine(results):
        total = None
        for r in reversed(range(zs)):
            blocks = [res[r * cap : (r + 1) * cap] for res in results]
            if ys == 2:
                away = [res[(zs + r) * cap : (zs + r + 1) * cap] for res in results]
                blocks.append(permute(jnp.concatenate(away, axis=0), across))
            block = jnp.concatenate(blocks, axis=0)
            sums = [
                lax.dot_general(pick[r], part, contract_first, preferred_element_type=jnp.float32)
                for part in cut(block)
            ]
            if total is not None:
                sums = [s + t.astype(jnp.float32) for s, t in zip(sums, total)]
            total = [s.astype(jnp.bfloat16) for s in sums]
            if r > 0:
                total = [permute(t, back) for t in total]
        return jnp.concatenate(total, axis=1)

    def both(weight):
        return weight[0], permute(weight[0], twin)

    gate_mats, up_mats, down_mats = both(w_gate), both(w_up), both(w_down)
    token_rows = dispatch(tokens, False)
    cot_rows = dispatch(cotangent, True)
    outs, saved = [], []
    for e in range(2):
        pre_gate = jnp.dot(token_rows[e], gate_mats[e], preferred_element_type=jnp.float32)
        pre_up = jnp.dot(token_rows[e], up_mats[e], preferred_element_type=jnp.float32)
        logistic = jax.nn.sigmoid(pre_gate)
        activated = pre_gate * logistic
        hidden = (activated * pre_up).astype(jnp.bfloat16)
        out = jnp.dot(hidden, down_mats[e], preferred_element_type=jnp.float32)
        outs.append((expert_gate[:, e].reshape(-1)[:, None] * out).astype(jnp.bfloat16))
        saved.append((pre_gate, pre_up, logistic, activated))
    moe_out = combine(outs)
    grads = []
    for e in range(2):
        pre_gate, pre_up, logistic, activated = saved[e]
        hidden_grad = lax.dot_general(cot_rows[e], down_mats[e], contract_last, preferred_element_type=jnp.float32)
        gate_grad = (hidden_grad * pre_up * logistic * (1.0 + pre_gate * (1.0 - logistic))).astype(jnp.bfloat16)
        up_grad = (hidden_grad * activated).astype(jnp.bfloat16)
        grad = lax.dot_general(
            gate_grad, gate_mats[e], contract_last, preferred_element_type=jnp.float32
        ) + lax.dot_general(up_grad, up_mats[e], contract_last, preferred_element_type=jnp.float32)
        grads.append(grad.astype(jnp.bfloat16))
    token_grad = combine(grads)
    return (moe_out, token_grad)


def solution(mesh):
    return jax.shard_map(
        per_device,
        mesh=mesh,
        in_specs=(
            P(("group", "wide"), None),
            P(("group", "wide"), None),
            P(("group", "wide"), None),
            P(("group", "wide"), None),
            P("wide", None, None),
            P("wide", None, None),
            P("wide", None, None),
        ),
        out_specs=(P(("group", "wide"), None), P(("group", "wide"), None)),
        check_vma=False,
    )
```

```python
import jax
import jax.numpy as jnp
from jax import lax
from jax.experimental import pallas as pl
from jax.experimental.pallas import tpu as pltpu
from jax.sharding import PartitionSpec as P

contract_last = (((1,), (1,)), ((), ()))
contract_first = (((0,), (0,)), ((), ()))
STREAMS = 2


def layout(wide):
    if wide == 16:
        return 4, 2, (0, 1, 3, 2)
    return wide // 2, 1, tuple(range(wide // 2))


def tie(value, *others):
    others = [other for other in others if other is not None]
    if not others:
        return value
    return pl.pallas_call(
        lambda *refs: None,
        out_shape=jax.ShapeDtypeStruct(value.shape, value.dtype),
        in_specs=[pl.BlockSpec(memory_space=pl.ANY)] * (1 + len(others)),
        out_specs=pl.BlockSpec(memory_space=pl.ANY),
        input_output_aliases={0: 0},
        name="tie",
    )(value, *others)


def whole_spec(shape):
    return pl.BlockSpec(shape, lambda *_: (0,) * len(shape))


ANYWHERE = pl.BlockSpec(memory_space=pl.ANY)


def params(mib):
    return pltpu.CompilerParams(vmem_limit_bytes=mib * 2**20)


def pick_rows(parts, pick, weight, refs):
    start = 0
    for part in parts:
        stop = start + part.shape[1]
        rows = jnp.dot(pick, part, preferred_element_type=jnp.float32)
        if weight is not None:
            rows = weight * rows
        rows = rows.astype(jnp.bfloat16)
        at = 0
        for ref in refs:
            ref[:, start:stop] = rows[at : at + ref.shape[0]]
            at += ref.shape[0]
        start = stop


def first_choice(experts, parts, width, cap, top, deps):
    rows = parts[0].shape[0]
    half = width // len(parts)
    count = experts.shape[0]
    chips = count // 2

    def body(experts, *refs):
        parts = refs[: len(refs) - chips - 2 - len(deps)]
        outs = refs[len(refs) - chips - 2 : len(refs) - 2]
        pick_ref, gated_ref = refs[-2:]
        routes = parts[0][0:16, half : half + rows].astype(jnp.float32)
        line = [routes[j : j + 1] for j in range(3 * top)]
        codes = [line[top + j] * 32.0 + line[2 * top + j] for j in range(top)]
        total = sum(codes[1:], codes[0])
        share = [code / total for code in codes]
        ids = [value.astype(jnp.int32) for value in line[:top]]
        hits, gates = [], []
        for k in range(count):
            hit, gate = jnp.zeros((1, rows), jnp.float32), jnp.zeros((1, rows), jnp.float32)
            for j in range(top):
                same = ids[j] == experts[k]
                hit = jnp.where(same, 1.0, hit)
                gate = jnp.where(same, gate + share[j], gate)
            hits.append(hit)
            gates.append(gate)
        stacked = jnp.concatenate(hits + [jnp.zeros((8 - count, rows), jnp.float32)], axis=0)
        upto = lax.broadcasted_iota(jnp.int32, (rows, rows), 0) <= lax.broadcasted_iota(jnp.int32, (rows, rows), 1)
        upto = jnp.where(upto, 1.0, 0.0).astype(jnp.bfloat16)
        spot = jnp.dot(stacked.astype(jnp.bfloat16), upto, preferred_element_type=jnp.float32).astype(jnp.int32) - 1
        slot = lax.broadcasted_iota(jnp.int32, (cap, rows), 0)
        picks, gated = [], []
        for k in range(count):
            chosen = jnp.where(slot == spot[k : k + 1], jnp.broadcast_to(hits[k], (cap, rows)), 0.0)
            picks.append(chosen)
            gated.append(chosen * gates[k])
        pick = jnp.concatenate(picks, axis=0).astype(jnp.bfloat16)
        pick_ref[...] = pick
        gated_ref[...] = jnp.concatenate(gated, axis=0)
        pick_rows([parts[0][:, :half]] + [part[...] for part in parts[1:]], pick, None, outs)

    rows_of = jax.ShapeDtypeStruct((2 * cap, width), jnp.bfloat16)
    results = pl.pallas_call(
        body,
        grid=(1,),
        in_specs=[pl.BlockSpec(memory_space=pltpu.SMEM)]
        + [whole_spec(part.shape) for part in parts]
        + [ANYWHERE] * len(deps),
        out_specs=[whole_spec((2 * cap, width))] * chips + [whole_spec((count * cap, rows))] * 2,
        out_shape=[rows_of] * chips
        + [
            jax.ShapeDtypeStruct((count * cap, rows), jnp.bfloat16),
            jax.ShapeDtypeStruct((count * cap, rows), jnp.float32),
        ],
        compiler_params=params(24),
        name="first_choice",
    )(experts, *parts, *deps)
    return results[:chips], results[chips:]


def next_choice(tables, parts, width, cap, deps):
    pick, gated = tables
    chips = pick.shape[0] // (2 * cap)

    def body(pick, gated, *refs):
        parts = refs[: len(refs) - chips - len(deps)]
        weight = jnp.sum(gated[...], axis=1, keepdims=True)
        pick_rows([part[...] for part in parts], pick[...], weight, refs[len(refs) - chips :])

    return pl.pallas_call(
        body,
        grid=(1,),
        in_specs=[whole_spec(pick.shape), whole_spec(gated.shape)]
        + [whole_spec(part.shape) for part in parts]
        + [ANYWHERE] * len(deps),
        out_specs=[whole_spec((2 * cap, width))] * chips,
        out_shape=[jax.ShapeDtypeStruct((2 * cap, width), jnp.bfloat16)] * chips,
        compiler_params=params(24),
        name="next_choice",
    )(pick, gated, *parts, *deps)


def back_sum(tables, weighted, pieces, came, part, parts, full=None):
    pick, gated = tables
    rows = pick.shape[1]
    width = pieces[0].shape[1]
    step = width // parts
    final = full is not None

    def body(mix, *refs):
        out = refs[-1]
        at, total = 0, None
        if came is not None:
            total = refs[len(pieces)][...].astype(jnp.float32)
        for ref in refs[: len(pieces)]:
            share = mix[at : at + ref.shape[0]]
            at += ref.shape[0]
            if weighted:
                upper = share.astype(jnp.bfloat16)
                shares = [upper, (share - upper.astype(jnp.float32)).astype(jnp.bfloat16)]
            else:
                shares = [share]
            for value in shares:
                more = lax.dot_general(value, ref[...], contract_first, preferred_element_type=jnp.float32)
                total = more if total is None else total + more
        out[...] = total.astype(jnp.bfloat16)

    mix = gated if weighted else pick
    operands = [mix, *pieces]
    specs = [whole_spec(mix.shape)] + [pl.BlockSpec((piece.shape[0], step), lambda g: (0, part)) for piece in pieces]
    if came is not None:
        operands.append(came)
        specs.append(whole_spec((rows, step)))
    aliases = {}
    if final and part > 0:
        aliases = {len(operands): 0}
        operands.append(full)
        specs.append(ANYWHERE)
    return pl.pallas_call(
        body,
        grid=(1,),
        in_specs=specs,
        out_specs=pl.BlockSpec((rows, step), lambda g: (0, part if final else 0)),
        out_shape=jax.ShapeDtypeStruct((rows, width if final else step), jnp.bfloat16),
        input_output_aliases=aliases,
        compiler_params=params(24),
        name="back_sum",
    )(*operands)


TILE = 256
WIDE_TILE = 1024


def expert_call(body, pieces, extras, weights, scratch, more_outs, cap, width, hidden, name, deps):
    firsts, seconds = hidden // TILE, width // WIDE_TILE
    total = len(pieces) * cap

    def first(j):
        return jnp.minimum(j, firsts - 1)

    def second(j):
        return jnp.maximum(j - firsts, 0)

    def at(e, mine, index, last):
        return jnp.where(e == mine, index, 0 if mine else last)

    specs = [pl.BlockSpec(piece.shape, lambda e, j: (0, 0), pipeline_mode=pl.Buffered(1)) for piece in pieces]
    specs += [pl.BlockSpec((1, total, TILE), lambda e, j: (e, 0, first(j)))] * len(extras)
    operands = list(pieces) + list(extras)
    for pair, block, axis, stage in weights:
        for mine, weight in enumerate(pair):
            last = (firsts if stage == 0 else seconds) - 1

            def where(e, j, mine=mine, axis=axis, stage=stage, last=last):
                index = at(e, mine, first(j) if stage == 0 else second(j), last)
                return (index, 0) if axis == 0 else (0, index)

            specs.append(pl.BlockSpec(block, where))
            operands.append(weight)
    specs += [ANYWHERE] * len(deps)
    operands += deps
    out_specs = [pl.BlockSpec((cap, WIDE_TILE), lambda e, j: (e, second(j)))] * len(pieces)
    out_shape = [jax.ShapeDtypeStruct((2 * cap, width), jnp.bfloat16)] * len(pieces)
    out_specs += [pl.BlockSpec((1, total, TILE), lambda e, j: (e, 0, first(j)))] * len(more_outs)
    out_shape += more_outs
    size = 6 * total * width * hidden * 2
    return pl.pallas_call(
        body,
        grid=(2, firsts + seconds),
        in_specs=specs,
        out_specs=out_specs,
        out_shape=out_shape,
        scratch_shapes=scratch,
        compiler_params=params(56),
        cost_estimate=pl.CostEstimate(flops=size, bytes_accessed=12 * width * hidden + 8 * total * width, transcendentals=0),
        name=name,
    )(*operands)


def put_rows(pieces, rows, e, cap):
    for i, piece in enumerate(pieces):
        rows[i * cap : (i + 1) * cap] = piece[pl.ds(pl.multiple_of(e * cap, 16), cap)]


def take_rows(outs, value, cap):
    for i, out in enumerate(outs):
        out[...] = value[i * cap : (i + 1) * cap]


def expert_forward(pieces, gates, ups, downs, cap, deps=()):
    width, hidden = gates[0].shape
    total = len(pieces) * cap
    firsts = hidden // TILE

    def body(*refs):
        n = len(pieces)
        pieces_in, refs = refs[:n], refs[n:]
        (gate0, gate1, up0, up1, down0, down1), refs = refs[:6], refs[6 + len(deps) :]
        outs, (slope, active, rows, inner) = refs[:n], refs[n:]
        e, j = pl.program_id(0), pl.program_id(1)

        @pl.when(j == 0)
        def _():
            put_rows(pieces_in, rows, e, cap)

        def enter(gate, up):
            pre_gate = jnp.dot(rows[...], gate[...], preferred_element_type=jnp.float32)
            pre_up = jnp.dot(rows[...], up[...], preferred_element_type=jnp.float32)
            logistic = jax.nn.sigmoid(pre_gate)
            activated = pre_gate * logistic
            active[0] = activated
            slope[0] = pre_up * logistic * (1.0 + pre_gate * (1.0 - logistic))
            for k in range(firsts):

                @pl.when(j == k)
                def _():
                    inner[:, k * TILE : (k + 1) * TILE] = (activated * pre_up).astype(jnp.bfloat16)

        def leave(down):
            value = jnp.dot(inner[...], down[...], preferred_element_type=jnp.float32)
            take_rows(outs, value.astype(jnp.bfloat16), cap)

        for mine, (gate, up, down) in enumerate(((gate0, up0, down0), (gate1, up1, down1))):
            pl.when((e == mine) & (j < firsts))(lambda gate=gate, up=up: enter(gate, up))
            pl.when((e == mine) & (j >= firsts))(lambda down=down: leave(down))

    saved = jax.ShapeDtypeStruct((2, total, hidden), jnp.float32)
    weights = [
        (gates, (width, TILE), 1, 0),
        (ups, (width, TILE), 1, 0),
        (downs, (hidden, WIDE_TILE), 1, 1),
    ]
    scratch = [pltpu.VMEM((total, width), jnp.bfloat16), pltpu.VMEM((total, hidden), jnp.bfloat16)]
    results = expert_call(
        body, pieces, [], weights, scratch, [saved, saved], cap, width, hidden, "expert_forward", list(deps)
    )
    return list(results[:-2]), list(results[-2:])


def expert_backward(pieces, saved, gates, ups, downs, cap, deps=()):
    width, hidden = gates[0].shape
    total = len(pieces) * cap
    firsts = hidden // TILE

    def body(*refs):
        n = len(pieces)
        pieces_in, refs = refs[:n], refs[n:]
        (slope, active), refs = refs[:2], refs[2:]
        (down0, down1, gate0, gate1, up0, up1), refs = refs[:6], refs[6 + len(deps) :]
        outs, (rows, gate_grad, up_grad) = refs[:n], refs[n:]
        e, j = pl.program_id(0), pl.program_id(1)

        @pl.when(j == 0)
        def _():
            put_rows(pieces_in, rows, e, cap)

        def enter(down):
            hidden_grad = lax.dot_general(rows[...], down[...], contract_last, preferred_element_type=jnp.float32)
            for k in range(firsts):

                @pl.when(j == k)
                def _():
                    gate_grad[:, k * TILE : (k + 1) * TILE] = (hidden_grad * slope[0]).astype(jnp.bfloat16)
                    up_grad[:, k * TILE : (k + 1) * TILE] = (hidden_grad * active[0]).astype(jnp.bfloat16)

        def leave(gate, up):
            value = lax.dot_general(gate_grad[...], gate[...], contract_last, preferred_element_type=jnp.float32)
            value += lax.dot_general(up_grad[...], up[...], contract_last, preferred_element_type=jnp.float32)
            take_rows(outs, value.astype(jnp.bfloat16), cap)

        for mine, (gate, up, down) in enumerate(((gate0, up0, down0), (gate1, up1, down1))):
            pl.when((e == mine) & (j < firsts))(lambda down=down: enter(down))
            pl.when((e == mine) & (j >= firsts))(lambda gate=gate, up=up: leave(gate, up))

    weights = [
        (downs, (TILE, width), 0, 0),
        (gates, (WIDE_TILE, hidden), 0, 1),
        (ups, (WIDE_TILE, hidden), 0, 1),
    ]
    scratch = [pltpu.VMEM((total, width), jnp.bfloat16)] + [pltpu.VMEM((total, hidden), jnp.bfloat16)] * 2
    return expert_call(
        body, pieces, list(saved), weights, scratch, [], cap, width, hidden, "expert_backward", list(deps)
    )


def per_device(tokens, cotangent, expert_ids, gate_codes, w_gate, w_up, w_down):
    wide = lax.axis_size("wide")
    rows, width = tokens.shape
    top = expert_ids.shape[1]
    cap = -(-3 * rows * top // (2 * wide) // 16) * 16
    zs, ys, ring = layout(wide)
    me = lax.axis_index("wide")
    core, col, my_z = me % 2, (me // 2) % ys, me // (2 * ys)

    def pairs(move):
        out = []
        for z in range(zs):
            for y in range(ys):
                for c in range(2):
                    tz, ty, tc = move(z, y, c)
                    out.append(((z * ys + y) * 2 + c, (tz * ys + ty) * 2 + tc))
        return out

    place = {z: i for i, z in enumerate(ring)}
    ahead = pairs(lambda z, y, c: (ring[(place[z] + 1) % zs], y, c))
    back = pairs(lambda z, y, c: (ring[(place[z] - 1) % zs], y, c))
    across = pairs(lambda z, y, c: (z, (y + 1) % ys, c))
    twin = pairs(lambda z, y, c: (z, y, 1 - c))

    def permute(value, perm):
        return lax.ppermute(value, "wide", perm)

    lanes = {}

    def send(lane, value, perm, depth=0):
        got = lanes.setdefault(lane, [])
        if depth and len(got) >= depth:
            value = tie(value, got[-depth])
        got.append(permute(value, perm))
        return got[-1]

    chip = my_z * ys + col
    experts = jnp.stack([2 * chip + core, 2 * chip + 1 - core])
    if ys == 2:
        there = my_z * ys + 1 - col
        experts = jnp.concatenate([experts, jnp.stack([2 * there + core, 2 * there + 1 - core])])
    slots = 2 * cap

    def cut(value):
        step = width // STREAMS
        return [value[:, i * step : (i + 1) * step] for i in range(STREAMS)]

    half = width // STREAMS
    routes = jnp.concatenate([expert_ids, gate_codes // 32, gate_codes % 32], axis=1).astype(jnp.bfloat16)
    routes = jnp.pad(routes.T, ((0, rows - 3 * top), (0, 0)))
    blocks = {
        "tokens": [[jnp.concatenate([tokens[:, :half], routes], axis=1)] + cut(tokens)[1:]],
        "cot": [cut(cotangent)],
    }
    own, other = {"tokens": [], "cot": []}, {"tokens": [], "cot": []}
    tables = []

    def came(lane, index):
        got = lanes.get(lane, [])
        return got[index] if index < len(got) else None

    def onward(name, early=(), late=()):
        parts = blocks[name][-1]
        parts[0] = tie(parts[0], *early)
        parts[-1] = tie(parts[-1], *late)
        first = 1 if len(blocks[name]) == 1 else 0
        blocks[name].append([send(i, part, ahead, first) for i, part in enumerate(parts)])

    def choose(name, r, deps=()):
        deps = [dep for dep in deps if dep is not None]
        if name == "tokens":
            chosen, found = first_choice(experts, blocks[name][r], width, cap, top, deps)
            tables.append(found)
        else:
            chosen = next_choice(tables[r], blocks[name][r], width, cap, deps)
        own[name].append(chosen[0])
        if ys == 2:
            other[name].append(send("y", chosen[1], across))

    def homeward(results, r, depth=2):
        return send("y", results[zs + r], across, depth) if ys == 2 else None

    def combine(results, weighted, far=None):
        total, steps = [None] * STREAMS, []
        for r in reversed(range(zs)):
            pieces = [results[r]]
            if ys == 2:
                pieces.append(far if r == zs - 1 and far is not None else homeward(results, r))
            if r == 0:
                full = tokens
                for i in range(STREAMS):
                    full = back_sum(tables[0], weighted, pieces, total[i], i, STREAMS, full)
                return full, steps
            for i in range(STREAMS):
                value = back_sum(tables[r], weighted, pieces, total[i], i, STREAMS)
                total[i] = send(i, value, back, 1 if r == zs - 1 else 0)
            steps.append(list(total))

    def both(weight):
        return weight[0], permute(weight[0], twin)

    gate_mats, up_mats, down_mats = both(w_gate), both(w_up), both(w_down)
    last = zs - 1
    choose("tokens", 0)
    choose("cot", 0)
    for r in range(1, zs):
        onward("tokens", [own["cot"][0] if r == 2 else own["tokens"][r - 2]] if r > 1 else [], [came("y", r - 2) if r > 1 else None])
        choose("tokens", r)
    for r in range(1, zs):
        if r == last:
            outs, saved = expert_forward(own["tokens"] + other["tokens"], gate_mats, up_mats, down_mats, cap)
        onward("cot", [own["tokens"][-1]] if r > 1 else [], [came("y", r + 1)] + ([outs[0]] if r == last else []))
        if r < last:
            choose("cot", r)
    far = homeward(outs, last)
    choose("cot", last, [outs[0]])
    moe_out, steps = combine(outs, True, far)
    deps = [came("y", 2 * zs + 1)] if ys == 2 else []
    grads = expert_backward(own["cot"] + other["cot"], saved, gate_mats, up_mats, down_mats, cap, deps + steps[0][:1])
    token_grad, _ = combine(grads, False)
    return (moe_out, token_grad)


def solution(mesh):
    return jax.shard_map(
        per_device,
        mesh=mesh,
        in_specs=(
            P(("group", "wide"), None),
            P(("group", "wide"), None),
            P(("group", "wide"), None),
            P(("group", "wide"), None),
            P("wide", None, None),
            P("wide", None, None),
            P("wide", None, None),
        ),
        out_specs=(P(("group", "wide"), None), P(("group", "wide"), None)),
        check_vma=False,
    )
```

```python
import jax
import jax.numpy as jnp
from jax import lax
from jax.experimental import pallas as pl
from jax.experimental.pallas import tpu as pltpu
from jax.sharding import PartitionSpec as P

contract_last = (((1,), (1,)), ((), ()))
contract_first = (((0,), (0,)), ((), ()))
STREAMS = 2


def layout(wide):
    if wide == 16:
        return 4, 2, (0, 1, 3, 2)
    return wide // 2, 1, tuple(range(wide // 2))


def tie(value, *others):
    others = [other for other in others if other is not None]
    if not others:
        return value
    return pl.pallas_call(
        lambda *refs: None,
        out_shape=jax.ShapeDtypeStruct(value.shape, value.dtype),
        in_specs=[pl.BlockSpec(memory_space=pl.ANY)] * (1 + len(others)),
        out_specs=pl.BlockSpec(memory_space=pl.ANY),
        input_output_aliases={0: 0},
        name="tie",
    )(value, *others)


def whole_spec(shape):
    return pl.BlockSpec(shape, lambda *_: (0,) * len(shape))


ANYWHERE = pl.BlockSpec(memory_space=pl.ANY)


def params(mib):
    return pltpu.CompilerParams(vmem_limit_bytes=mib * 2**20)


def pick_rows(parts, pick, weight, refs):
    start = 0
    for part in parts:
        stop = start + part.shape[1]
        rows = jnp.dot(pick, part, preferred_element_type=jnp.float32)
        if weight is not None:
            rows = weight * rows
        rows = rows.astype(jnp.bfloat16)
        at = 0
        for ref in refs:
            ref[:, start:stop] = rows[at : at + ref.shape[0]]
            at += ref.shape[0]
        start = stop


def first_choice(experts, parts, width, cap, top, deps):
    rows = parts[0].shape[0]
    half = width // len(parts)
    count = experts.shape[0]
    chips = count // 2

    def body(experts, *refs):
        parts = refs[: len(refs) - chips - 2 - len(deps)]
        outs = refs[len(refs) - chips - 2 : len(refs) - 2]
        pick_ref, gated_ref = refs[-2:]
        routes = parts[0][0:16, half : half + rows].astype(jnp.float32)
        line = [routes[j : j + 1] for j in range(3 * top)]
        codes = [line[top + j] * 32.0 + line[2 * top + j] for j in range(top)]
        total = sum(codes[1:], codes[0])
        share = [code / total for code in codes]
        ids = [value.astype(jnp.int32) for value in line[:top]]
        hits, gates = [], []
        for k in range(count):
            hit, gate = jnp.zeros((1, rows), jnp.float32), jnp.zeros((1, rows), jnp.float32)
            for j in range(top):
                same = ids[j] == experts[k]
                hit = jnp.where(same, 1.0, hit)
                gate = jnp.where(same, gate + share[j], gate)
            hits.append(hit)
            gates.append(gate)
        stacked = jnp.concatenate(hits + [jnp.zeros((8 - count, rows), jnp.float32)], axis=0)
        upto = lax.broadcasted_iota(jnp.int32, (rows, rows), 0) <= lax.broadcasted_iota(jnp.int32, (rows, rows), 1)
        upto = jnp.where(upto, 1.0, 0.0).astype(jnp.bfloat16)
        spot = jnp.dot(stacked.astype(jnp.bfloat16), upto, preferred_element_type=jnp.float32).astype(jnp.int32) - 1
        slot = lax.broadcasted_iota(jnp.int32, (cap, rows), 0)
        picks, gated = [], []
        for k in range(count):
            chosen = jnp.where(slot == spot[k : k + 1], jnp.broadcast_to(hits[k], (cap, rows)), 0.0)
            picks.append(chosen)
            gated.append(chosen * gates[k])
        pick = jnp.concatenate(picks, axis=0).astype(jnp.bfloat16)
        pick_ref[...] = pick
        gated_ref[...] = jnp.concatenate(gated, axis=0)
        pick_rows([parts[0][:, :half]] + [part[...] for part in parts[1:]], pick, None, outs)

    rows_of = jax.ShapeDtypeStruct((2 * cap, width), jnp.bfloat16)
    results = pl.pallas_call(
        body,
        grid=(1,),
        in_specs=[pl.BlockSpec(memory_space=pltpu.SMEM)]
        + [whole_spec(part.shape) for part in parts]
        + [ANYWHERE] * len(deps),
        out_specs=[whole_spec((2 * cap, width))] * chips + [whole_spec((count * cap, rows))] * 2,
        out_shape=[rows_of] * chips
        + [
            jax.ShapeDtypeStruct((count * cap, rows), jnp.bfloat16),
            jax.ShapeDtypeStruct((count * cap, rows), jnp.float32),
        ],
        compiler_params=params(24),
        name="first_choice",
    )(experts, *parts, *deps)
    return results[:chips], results[chips:]


def next_choice(tables, parts, width, cap, deps):
    pick, gated = tables
    chips = pick.shape[0] // (2 * cap)

    def body(pick, gated, *refs):
        parts = refs[: len(refs) - chips - len(deps)]
        weight = jnp.sum(gated[...], axis=1, keepdims=True)
        pick_rows([part[...] for part in parts], pick[...], weight, refs[len(refs) - chips :])

    return pl.pallas_call(
        body,
        grid=(1,),
        in_specs=[whole_spec(pick.shape), whole_spec(gated.shape)]
        + [whole_spec(part.shape) for part in parts]
        + [ANYWHERE] * len(deps),
        out_specs=[whole_spec((2 * cap, width))] * chips,
        out_shape=[jax.ShapeDtypeStruct((2 * cap, width), jnp.bfloat16)] * chips,
        compiler_params=params(24),
        name="next_choice",
    )(pick, gated, *parts, *deps)


def back_sum(tables, weighted, pieces, came, part, parts, full=None):
    pick, gated = tables
    rows = pick.shape[1]
    width = pieces[0].shape[1]
    step = width // parts
    final = full is not None

    def body(mix, *refs):
        out = refs[-1]
        at, total = 0, None
        if came is not None:
            total = refs[len(pieces)][...].astype(jnp.float32)
        for ref in refs[: len(pieces)]:
            share = mix[at : at + ref.shape[0]]
            at += ref.shape[0]
            if weighted:
                upper = share.astype(jnp.bfloat16)
                shares = [upper, (share - upper.astype(jnp.float32)).astype(jnp.bfloat16)]
            else:
                shares = [share]
            for value in shares:
                more = lax.dot_general(value, ref[...], contract_first, preferred_element_type=jnp.float32)
                total = more if total is None else total + more
        out[...] = total.astype(jnp.bfloat16)

    mix = gated if weighted else pick
    operands = [mix, *pieces]
    specs = [whole_spec(mix.shape)] + [pl.BlockSpec((piece.shape[0], step), lambda g: (0, part)) for piece in pieces]
    if came is not None:
        operands.append(came)
        specs.append(whole_spec((rows, step)))
    aliases = {}
    if final and part > 0:
        aliases = {len(operands): 0}
        operands.append(full)
        specs.append(ANYWHERE)
    return pl.pallas_call(
        body,
        grid=(1,),
        in_specs=specs,
        out_specs=pl.BlockSpec((rows, step), lambda g: (0, part if final else 0)),
        out_shape=jax.ShapeDtypeStruct((rows, width if final else step), jnp.bfloat16),
        input_output_aliases=aliases,
        compiler_params=params(24),
        name="back_sum",
    )(*operands)


TILE = 256
WIDE_TILE = 1024


def expert_call(body, pieces, extras, weights, scratch, more_outs, cap, width, hidden, name, deps):
    firsts, seconds = hidden // TILE, width // WIDE_TILE
    total = len(pieces) * cap

    def first(j):
        return jnp.minimum(j, firsts - 1)

    def second(j):
        return jnp.maximum(j - firsts, 0)

    def at(e, mine, index, last):
        return jnp.where(e == mine, index, 0 if mine else last)

    specs = [pl.BlockSpec(piece.shape, lambda e, j: (0, 0), pipeline_mode=pl.Buffered(1)) for piece in pieces]
    specs += [pl.BlockSpec((1, total, TILE), lambda e, j: (e, 0, first(j)))] * len(extras)
    operands = list(pieces) + list(extras)
    for pair, block, axis, stage in weights:
        for mine, weight in enumerate(pair):
            last = (firsts if stage == 0 else seconds) - 1

            def where(e, j, mine=mine, axis=axis, stage=stage, last=last):
                index = at(e, mine, first(j) if stage == 0 else second(j), last)
                return (index, 0) if axis == 0 else (0, index)

            specs.append(pl.BlockSpec(block, where))
            operands.append(weight)
    specs += [ANYWHERE] * len(deps)
    operands += deps
    out_specs = [pl.BlockSpec((cap, WIDE_TILE), lambda e, j: (e, second(j)))] * len(pieces)
    out_shape = [jax.ShapeDtypeStruct((2 * cap, width), jnp.bfloat16)] * len(pieces)
    out_specs += [pl.BlockSpec((1, total, TILE), lambda e, j: (e, 0, first(j)))] * len(more_outs)
    out_shape += more_outs
    size = 6 * total * width * hidden * 2
    return pl.pallas_call(
        body,
        grid=(2, firsts + seconds),
        in_specs=specs,
        out_specs=out_specs,
        out_shape=out_shape,
        scratch_shapes=scratch,
        compiler_params=params(56),
        cost_estimate=pl.CostEstimate(flops=size, bytes_accessed=12 * width * hidden + 8 * total * width, transcendentals=0),
        name=name,
    )(*operands)


def put_rows(pieces, rows, e, cap):
    for i, piece in enumerate(pieces):
        rows[i * cap : (i + 1) * cap] = piece[pl.ds(pl.multiple_of(e * cap, 16), cap)]


def take_rows(outs, value, cap):
    for i, out in enumerate(outs):
        out[...] = value[i * cap : (i + 1) * cap]


def expert_forward(pieces, gates, ups, downs, cap, deps=()):
    width, hidden = gates[0].shape
    total = len(pieces) * cap
    firsts = hidden // TILE

    def body(*refs):
        n = len(pieces)
        pieces_in, refs = refs[:n], refs[n:]
        (gate0, gate1, up0, up1, down0, down1), refs = refs[:6], refs[6 + len(deps) :]
        outs, (slope, active, rows, inner) = refs[:n], refs[n:]
        e, j = pl.program_id(0), pl.program_id(1)

        @pl.when(j == 0)
        def _():
            put_rows(pieces_in, rows, e, cap)

        def enter(gate, up):
            pre_gate = jnp.dot(rows[...], gate[...], preferred_element_type=jnp.float32)
            pre_up = jnp.dot(rows[...], up[...], preferred_element_type=jnp.float32)
            logistic = jax.nn.sigmoid(pre_gate)
            activated = pre_gate * logistic
            active[0] = activated
            slope[0] = pre_up * logistic * (1.0 + pre_gate * (1.0 - logistic))
            for k in range(firsts):

                @pl.when(j == k)
                def _():
                    inner[:, k * TILE : (k + 1) * TILE] = (activated * pre_up).astype(jnp.bfloat16)

        def leave(down):
            value = jnp.dot(inner[...], down[...], preferred_element_type=jnp.float32)
            take_rows(outs, value.astype(jnp.bfloat16), cap)

        for mine, (gate, up, down) in enumerate(((gate0, up0, down0), (gate1, up1, down1))):
            pl.when((e == mine) & (j < firsts))(lambda gate=gate, up=up: enter(gate, up))
            pl.when((e == mine) & (j >= firsts))(lambda down=down: leave(down))

    saved = jax.ShapeDtypeStruct((2, total, hidden), jnp.float32)
    weights = [
        (gates, (width, TILE), 1, 0),
        (ups, (width, TILE), 1, 0),
        (downs, (hidden, WIDE_TILE), 1, 1),
    ]
    scratch = [pltpu.VMEM((total, width), jnp.bfloat16), pltpu.VMEM((total, hidden), jnp.bfloat16)]
    results = expert_call(
        body, pieces, [], weights, scratch, [saved, saved], cap, width, hidden, "expert_forward", list(deps)
    )
    return list(results[:-2]), list(results[-2:])


def expert_backward(pieces, saved, gates, ups, downs, cap, deps=()):
    width, hidden = gates[0].shape
    total = len(pieces) * cap
    firsts = hidden // TILE

    def body(*refs):
        n = len(pieces)
        pieces_in, refs = refs[:n], refs[n:]
        (slope, active), refs = refs[:2], refs[2:]
        (down0, down1, gate0, gate1, up0, up1), refs = refs[:6], refs[6 + len(deps) :]
        outs, (rows, gate_grad, up_grad) = refs[:n], refs[n:]
        e, j = pl.program_id(0), pl.program_id(1)

        @pl.when(j == 0)
        def _():
            put_rows(pieces_in, rows, e, cap)

        def enter(down):
            hidden_grad = lax.dot_general(rows[...], down[...], contract_last, preferred_element_type=jnp.float32)
            for k in range(firsts):

                @pl.when(j == k)
                def _():
                    gate_grad[:, k * TILE : (k + 1) * TILE] = (hidden_grad * slope[0]).astype(jnp.bfloat16)
                    up_grad[:, k * TILE : (k + 1) * TILE] = (hidden_grad * active[0]).astype(jnp.bfloat16)

        def leave(gate, up):
            value = lax.dot_general(gate_grad[...], gate[...], contract_last, preferred_element_type=jnp.float32)
            value += lax.dot_general(up_grad[...], up[...], contract_last, preferred_element_type=jnp.float32)
            take_rows(outs, value.astype(jnp.bfloat16), cap)

        for mine, (gate, up, down) in enumerate(((gate0, up0, down0), (gate1, up1, down1))):
            pl.when((e == mine) & (j < firsts))(lambda down=down: enter(down))
            pl.when((e == mine) & (j >= firsts))(lambda gate=gate, up=up: leave(gate, up))

    weights = [
        (downs, (TILE, width), 0, 0),
        (gates, (WIDE_TILE, hidden), 0, 1),
        (ups, (WIDE_TILE, hidden), 0, 1),
    ]
    scratch = [pltpu.VMEM((total, width), jnp.bfloat16)] + [pltpu.VMEM((total, hidden), jnp.bfloat16)] * 2
    return expert_call(
        body, pieces, list(saved), weights, scratch, [], cap, width, hidden, "expert_backward", list(deps)
    )


def per_device(tokens, cotangent, expert_ids, gate_codes, w_gate, w_up, w_down):
    wide = lax.axis_size("wide")
    rows, width = tokens.shape
    top = expert_ids.shape[1]
    cap = -(-3 * rows * top // (2 * wide) // 16) * 16
    zs, ys, ring = layout(wide)
    me = lax.axis_index("wide")
    core, col, my_z = me % 2, (me // 2) % ys, me // (2 * ys)

    def pairs(move):
        out = []
        for z in range(zs):
            for y in range(ys):
                for c in range(2):
                    tz, ty, tc = move(z, y, c)
                    out.append(((z * ys + y) * 2 + c, (tz * ys + ty) * 2 + tc))
        return out

    place = {z: i for i, z in enumerate(ring)}
    ahead = pairs(lambda z, y, c: (ring[(place[z] + 1) % zs], y, c))
    back = pairs(lambda z, y, c: (ring[(place[z] - 1) % zs], y, c))
    across = pairs(lambda z, y, c: (z, (y + 1) % ys, c))
    twin = pairs(lambda z, y, c: (z, y, 1 - c))

    def permute(value, perm):
        return lax.ppermute(value, "wide", perm)

    lanes = {}

    def send(lane, value, perm, depth=0):
        got = lanes.setdefault(lane, [])
        if depth and len(got) >= depth:
            value = tie(value, got[-depth])
        got.append(permute(value, perm))
        return got[-1]

    chip = my_z * ys + col
    experts = jnp.stack([2 * chip + core, 2 * chip + 1 - core])
    if ys == 2:
        there = my_z * ys + 1 - col
        experts = jnp.concatenate([experts, jnp.stack([2 * there + core, 2 * there + 1 - core])])
    slots = 2 * cap

    def cut(value):
        step = width // STREAMS
        return [value[:, i * step : (i + 1) * step] for i in range(STREAMS)]

    half = width // STREAMS
    routes = jnp.concatenate([expert_ids, gate_codes // 32, gate_codes % 32], axis=1).astype(jnp.bfloat16)
    routes = jnp.pad(routes.T, ((0, rows - 3 * top), (0, 0)))
    blocks = {
        "tokens": [[jnp.concatenate([tokens[:, :half], routes], axis=1)] + cut(tokens)[1:]],
        "cot": [cut(cotangent)],
    }
    own, other = {"tokens": [], "cot": []}, {"tokens": [], "cot": []}
    tables = []

    def came(lane, index):
        got = lanes.get(lane, [])
        return got[index] if index < len(got) else None

    def onward(name, early=(), late=()):
        parts = blocks[name][-1]
        parts[0] = tie(parts[0], *early)
        parts[-1] = tie(parts[-1], *late)
        first = 1 if len(blocks[name]) == 1 else 0
        blocks[name].append([send(i, part, ahead, first) for i, part in enumerate(parts)])

    def choose(name, r, deps=()):
        deps = [dep for dep in deps if dep is not None]
        if name == "tokens":
            chosen, found = first_choice(experts, blocks[name][r], width, cap, top, deps)
            tables.append(found)
        else:
            chosen = next_choice(tables[r], blocks[name][r], width, cap, deps)
        own[name].append(chosen[0])
        if ys == 2:
            other[name].append(send("y", chosen[1], across))

    def homeward(results, r, depth=2):
        return send("y", results[zs + r], across, depth) if ys == 2 else None

    def combine(results, weighted, far=None):
        total, steps = [None] * STREAMS, []
        for r in reversed(range(zs)):
            pieces = [results[r]]
            if ys == 2:
                pieces.append(far if r == zs - 1 and far is not None else homeward(results, r))
            if r == 0:
                full = tokens
                for i in range(STREAMS):
                    full = back_sum(tables[0], weighted, pieces, total[i], i, STREAMS, full)
                return full, steps
            for i in range(STREAMS):
                value = back_sum(tables[r], weighted, pieces, total[i], i, STREAMS)
                total[i] = send(i, value, back, 1 if r == zs - 1 else 0)
            steps.append(list(total))

    def both(weight):
        return weight[0], permute(weight[0], twin)

    gate_mats, up_mats, down_mats = both(w_gate), both(w_up), both(w_down)
    twins = [gate_mats[1], up_mats[1], down_mats[1]]
    last = zs - 1
    choose("tokens", 0)
    choose("cot", 0)
    for r in range(1, zs):
        onward("tokens", [own["cot"][0] if r == 2 else own["tokens"][r - 2]] if r > 1 else [], [came("y", r - 2), *(twins if r == 2 else [])] if r > 1 else [])
        choose("tokens", r)
    for r in range(1, zs):
        if r == last:
            outs, saved = expert_forward(own["tokens"] + other["tokens"], gate_mats, up_mats, down_mats, cap)
        onward("cot", [own["tokens"][-1]] if r > 1 else [], [came("y", r + 1)] + ([outs[0]] if r == last else []))
        if r < last:
            choose("cot", r)
    far = homeward(outs, last)
    choose("cot", last, [outs[0]])
    moe_out, steps = combine(outs, True, far)
    deps = [came("y", 2 * zs + 1)] if ys == 2 else []
    grads = expert_backward(own["cot"] + other["cot"], saved, gate_mats, up_mats, down_mats, cap, deps + steps[0][:1])
    token_grad, _ = combine(grads, False)
    return (moe_out, token_grad)


def solution(mesh):
    return jax.shard_map(
        per_device,
        mesh=mesh,
        in_specs=(
            P(("group", "wide"), None),
            P(("group", "wide"), None),
            P(("group", "wide"), None),
            P(("group", "wide"), None),
            P("wide", None, None),
            P("wide", None, None),
            P("wide", None, None),
        ),
        out_specs=(P(("group", "wide"), None), P(("group", "wide"), None)),
        check_vma=False,
    )
```

```python
import jax
import jax.numpy as jnp
from jax import lax
from jax.experimental import pallas as pl
from jax.experimental.pallas import tpu as pltpu
from jax.sharding import PartitionSpec as P

contract_last = (((1,), (1,)), ((), ()))
contract_first = (((0,), (0,)), ((), ()))
STREAMS = 2


def layout(wide):
    if wide == 16:
        return 4, 2, (0, 1, 3, 2)
    return wide // 2, 1, tuple(range(wide // 2))


def tie(value, *others):
    others = [other for other in others if other is not None]
    if not others:
        return value
    return pl.pallas_call(
        lambda *refs: None,
        out_shape=jax.ShapeDtypeStruct(value.shape, value.dtype),
        in_specs=[pl.BlockSpec(memory_space=pl.ANY)] * (1 + len(others)),
        out_specs=pl.BlockSpec(memory_space=pl.ANY),
        input_output_aliases={0: 0},
        name="tie",
    )(value, *others)


def whole_spec(shape):
    return pl.BlockSpec(shape, lambda *_: (0,) * len(shape))


ANYWHERE = pl.BlockSpec(memory_space=pl.ANY)


def params(mib):
    return pltpu.CompilerParams(vmem_limit_bytes=mib * 2**20)


def pick_rows(parts, pick, weight, refs):
    start = 0
    for part in parts:
        stop = start + part.shape[1]
        rows = jnp.dot(pick, part, preferred_element_type=jnp.float32)
        if weight is not None:
            rows = weight * rows
        rows = rows.astype(jnp.bfloat16)
        at = 0
        for ref in refs:
            ref[:, start:stop] = rows[at : at + ref.shape[0]]
            at += ref.shape[0]
        start = stop


def first_choice(experts, parts, width, cap, top, deps):
    rows = parts[0].shape[0]
    half = width // len(parts)
    count = experts.shape[0]
    chips = count // 2

    def body(experts, *refs):
        parts = refs[: len(refs) - chips - 2 - len(deps)]
        outs = refs[len(refs) - chips - 2 : len(refs) - 2]
        pick_ref, gated_ref = refs[-2:]
        routes = parts[0][0:16, half : half + rows].astype(jnp.float32)
        line = [routes[j : j + 1] for j in range(3 * top)]
        codes = [line[top + j] * 32.0 + line[2 * top + j] for j in range(top)]
        total = sum(codes[1:], codes[0])
        share = [code / total for code in codes]
        ids = [value.astype(jnp.int32) for value in line[:top]]
        hits, gates = [], []
        for k in range(count):
            hit, gate = jnp.zeros((1, rows), jnp.float32), jnp.zeros((1, rows), jnp.float32)
            for j in range(top):
                same = ids[j] == experts[k]
                hit = jnp.where(same, 1.0, hit)
                gate = jnp.where(same, gate + share[j], gate)
            hits.append(hit)
            gates.append(gate)
        stacked = jnp.concatenate(hits + [jnp.zeros((8 - count, rows), jnp.float32)], axis=0)
        upto = lax.broadcasted_iota(jnp.int32, (rows, rows), 0) <= lax.broadcasted_iota(jnp.int32, (rows, rows), 1)
        upto = jnp.where(upto, 1.0, 0.0).astype(jnp.bfloat16)
        spot = jnp.dot(stacked.astype(jnp.bfloat16), upto, preferred_element_type=jnp.float32).astype(jnp.int32) - 1
        slot = lax.broadcasted_iota(jnp.int32, (cap, rows), 0)
        picks, gated = [], []
        for k in range(count):
            chosen = jnp.where(slot == spot[k : k + 1], jnp.broadcast_to(hits[k], (cap, rows)), 0.0)
            picks.append(chosen)
            gated.append(chosen * gates[k])
        pick = jnp.concatenate(picks, axis=0).astype(jnp.bfloat16)
        pick_ref[...] = pick
        gated_ref[...] = jnp.concatenate(gated, axis=0)
        pick_rows([parts[0][:, :half]] + [part[...] for part in parts[1:]], pick, None, outs)

    rows_of = jax.ShapeDtypeStruct((2 * cap, width), jnp.bfloat16)
    results = pl.pallas_call(
        body,
        grid=(1,),
        in_specs=[pl.BlockSpec(memory_space=pltpu.SMEM)]
        + [whole_spec(part.shape) for part in parts]
        + [ANYWHERE] * len(deps),
        out_specs=[whole_spec((2 * cap, width))] * chips + [whole_spec((count * cap, rows))] * 2,
        out_shape=[rows_of] * chips
        + [
            jax.ShapeDtypeStruct((count * cap, rows), jnp.bfloat16),
            jax.ShapeDtypeStruct((count * cap, rows), jnp.float32),
        ],
        compiler_params=params(24),
        name="first_choice",
    )(experts, *parts, *deps)
    return results[:chips], results[chips:]


def next_choice(tables, parts, width, cap, deps):
    pick, gated = tables
    chips = pick.shape[0] // (2 * cap)

    def body(pick, gated, *refs):
        parts = refs[: len(refs) - chips - len(deps)]
        weight = jnp.sum(gated[...], axis=1, keepdims=True)
        pick_rows([part[...] for part in parts], pick[...], weight, refs[len(refs) - chips :])

    return pl.pallas_call(
        body,
        grid=(1,),
        in_specs=[whole_spec(pick.shape), whole_spec(gated.shape)]
        + [whole_spec(part.shape) for part in parts]
        + [ANYWHERE] * len(deps),
        out_specs=[whole_spec((2 * cap, width))] * chips,
        out_shape=[jax.ShapeDtypeStruct((2 * cap, width), jnp.bfloat16)] * chips,
        compiler_params=params(24),
        name="next_choice",
    )(pick, gated, *parts, *deps)


def back_sum(tables, weighted, pieces, came, part, parts, full=None):
    pick, gated = tables
    rows = pick.shape[1]
    width = pieces[0].shape[1]
    step = width // parts
    final = full is not None

    def body(mix, *refs):
        out = refs[-1]
        at, total = 0, None
        if came is not None:
            total = refs[len(pieces)][...].astype(jnp.float32)
        for ref in refs[: len(pieces)]:
            share = mix[at : at + ref.shape[0]]
            at += ref.shape[0]
            if weighted:
                upper = share.astype(jnp.bfloat16)
                shares = [upper, (share - upper.astype(jnp.float32)).astype(jnp.bfloat16)]
            else:
                shares = [share]
            for value in shares:
                more = lax.dot_general(value, ref[...], contract_first, preferred_element_type=jnp.float32)
                total = more if total is None else total + more
        out[...] = total.astype(jnp.bfloat16)

    mix = gated if weighted else pick
    operands = [mix, *pieces]
    specs = [whole_spec(mix.shape)] + [pl.BlockSpec((piece.shape[0], step), lambda g: (0, part)) for piece in pieces]
    if came is not None:
        operands.append(came)
        specs.append(whole_spec((rows, step)))
    aliases = {}
    if final and part > 0:
        aliases = {len(operands): 0}
        operands.append(full)
        specs.append(ANYWHERE)
    return pl.pallas_call(
        body,
        grid=(1,),
        in_specs=specs,
        out_specs=pl.BlockSpec((rows, step), lambda g: (0, part if final else 0)),
        out_shape=jax.ShapeDtypeStruct((rows, width if final else step), jnp.bfloat16),
        input_output_aliases=aliases,
        compiler_params=params(24),
        name="back_sum",
    )(*operands)


TILE = 256
WIDE_TILE = 1024


def expert_call(body, pieces, extras, weights, scratch, more_outs, cap, width, hidden, name, deps):
    firsts, seconds = hidden // TILE, width // WIDE_TILE
    total = len(pieces) * cap

    def first(j):
        return jnp.minimum(j, firsts - 1)

    def second(j):
        return jnp.maximum(j - firsts, 0)

    def at(e, mine, index, last):
        return jnp.where(e == mine, index, 0 if mine else last)

    specs = [pl.BlockSpec(piece.shape, lambda e, j: (0, 0), pipeline_mode=pl.Buffered(1)) for piece in pieces]
    specs += [pl.BlockSpec((1, total, TILE), lambda e, j: (e, 0, first(j)))] * len(extras)
    operands = list(pieces) + list(extras)
    for pair, block, axis, stage in weights:
        for mine, weight in enumerate(pair):
            last = (firsts if stage == 0 else seconds) - 1

            def where(e, j, mine=mine, axis=axis, stage=stage, last=last):
                index = at(e, mine, first(j) if stage == 0 else second(j), last)
                return (index, 0) if axis == 0 else (0, index)

            specs.append(pl.BlockSpec(block, where))
            operands.append(weight)
    specs += [ANYWHERE] * len(deps)
    operands += deps
    out_specs = [pl.BlockSpec((cap, WIDE_TILE), lambda e, j: (e, second(j)))] * len(pieces)
    out_shape = [jax.ShapeDtypeStruct((2 * cap, width), jnp.bfloat16)] * len(pieces)
    out_specs += [pl.BlockSpec((1, total, TILE), lambda e, j: (e, 0, first(j)))] * len(more_outs)
    out_shape += more_outs
    size = 6 * total * width * hidden * 2
    return pl.pallas_call(
        body,
        grid=(2, firsts + seconds),
        in_specs=specs,
        out_specs=out_specs,
        out_shape=out_shape,
        scratch_shapes=scratch,
        compiler_params=params(56),
        cost_estimate=pl.CostEstimate(flops=size, bytes_accessed=12 * width * hidden + 8 * total * width, transcendentals=0),
        name=name,
    )(*operands)


def put_rows(pieces, rows, e, cap):
    for i, piece in enumerate(pieces):
        rows[i * cap : (i + 1) * cap] = piece[pl.ds(pl.multiple_of(e * cap, 16), cap)]


def take_rows(outs, value, cap):
    for i, out in enumerate(outs):
        out[...] = value[i * cap : (i + 1) * cap]


def expert_forward(pieces, gates, ups, downs, cap, deps=()):
    width, hidden = gates[0].shape
    total = len(pieces) * cap
    firsts = hidden // TILE

    def body(*refs):
        n = len(pieces)
        pieces_in, refs = refs[:n], refs[n:]
        (gate0, gate1, up0, up1, down0, down1), refs = refs[:6], refs[6 + len(deps) :]
        outs, (slope, active, rows, inner) = refs[:n], refs[n:]
        e, j = pl.program_id(0), pl.program_id(1)

        @pl.when(j == 0)
        def _():
            put_rows(pieces_in, rows, e, cap)

        def enter(gate, up):
            pre_gate = jnp.dot(rows[...], gate[...], preferred_element_type=jnp.float32)
            pre_up = jnp.dot(rows[...], up[...], preferred_element_type=jnp.float32)
            logistic = jax.nn.sigmoid(pre_gate)
            activated = pre_gate * logistic
            active[0] = activated
            slope[0] = pre_up * logistic * (1.0 + pre_gate * (1.0 - logistic))
            for k in range(firsts):

                @pl.when(j == k)
                def _():
                    inner[:, k * TILE : (k + 1) * TILE] = (activated * pre_up).astype(jnp.bfloat16)

        def leave(down):
            value = jnp.dot(inner[...], down[...], preferred_element_type=jnp.float32)
            take_rows(outs, value.astype(jnp.bfloat16), cap)

        for mine, (gate, up, down) in enumerate(((gate0, up0, down0), (gate1, up1, down1))):
            pl.when((e == mine) & (j < firsts))(lambda gate=gate, up=up: enter(gate, up))
            pl.when((e == mine) & (j >= firsts))(lambda down=down: leave(down))

    saved = jax.ShapeDtypeStruct((2, total, hidden), jnp.float32)
    weights = [
        (gates, (width, TILE), 1, 0),
        (ups, (width, TILE), 1, 0),
        (downs, (hidden, WIDE_TILE), 1, 1),
    ]
    scratch = [pltpu.VMEM((total, width), jnp.bfloat16), pltpu.VMEM((total, hidden), jnp.bfloat16)]
    results = expert_call(
        body, pieces, [], weights, scratch, [saved, saved], cap, width, hidden, "expert_forward", list(deps)
    )
    return list(results[:-2]), list(results[-2:])


def expert_backward(pieces, saved, gates, ups, downs, cap, deps=()):
    width, hidden = gates[0].shape
    total = len(pieces) * cap
    firsts = hidden // TILE

    def body(*refs):
        n = len(pieces)
        pieces_in, refs = refs[:n], refs[n:]
        (slope, active), refs = refs[:2], refs[2:]
        (down0, down1, gate0, gate1, up0, up1), refs = refs[:6], refs[6 + len(deps) :]
        outs, (rows, gate_grad, up_grad) = refs[:n], refs[n:]
        e, j = pl.program_id(0), pl.program_id(1)

        @pl.when(j == 0)
        def _():
            put_rows(pieces_in, rows, e, cap)

        def enter(down):
            hidden_grad = lax.dot_general(rows[...], down[...], contract_last, preferred_element_type=jnp.float32)
            for k in range(firsts):

                @pl.when(j == k)
                def _():
                    gate_grad[:, k * TILE : (k + 1) * TILE] = (hidden_grad * slope[0]).astype(jnp.bfloat16)
                    up_grad[:, k * TILE : (k + 1) * TILE] = (hidden_grad * active[0]).astype(jnp.bfloat16)

        def leave(gate, up):
            value = lax.dot_general(gate_grad[...], gate[...], contract_last, preferred_element_type=jnp.float32)
            value += lax.dot_general(up_grad[...], up[...], contract_last, preferred_element_type=jnp.float32)
            take_rows(outs, value.astype(jnp.bfloat16), cap)

        for mine, (gate, up, down) in enumerate(((gate0, up0, down0), (gate1, up1, down1))):
            pl.when((e == mine) & (j < firsts))(lambda down=down: enter(down))
            pl.when((e == mine) & (j >= firsts))(lambda gate=gate, up=up: leave(gate, up))

    weights = [
        (downs, (TILE, width), 0, 0),
        (gates, (WIDE_TILE, hidden), 0, 1),
        (ups, (WIDE_TILE, hidden), 0, 1),
    ]
    scratch = [pltpu.VMEM((total, width), jnp.bfloat16)] + [pltpu.VMEM((total, hidden), jnp.bfloat16)] * 2
    return expert_call(
        body, pieces, list(saved), weights, scratch, [], cap, width, hidden, "expert_backward", list(deps)
    )


def per_device(tokens, cotangent, expert_ids, gate_codes, w_gate, w_up, w_down):
    wide = lax.axis_size("wide")
    rows, width = tokens.shape
    top = expert_ids.shape[1]
    cap = -(-3 * rows * top // (2 * wide) // 16) * 16
    zs, ys, ring = layout(wide)
    me = lax.axis_index("wide")
    core, col, my_z = me % 2, (me // 2) % ys, me // (2 * ys)

    def pairs(move):
        out = []
        for z in range(zs):
            for y in range(ys):
                for c in range(2):
                    tz, ty, tc = move(z, y, c)
                    out.append(((z * ys + y) * 2 + c, (tz * ys + ty) * 2 + tc))
        return out

    place = {z: i for i, z in enumerate(ring)}
    ahead = pairs(lambda z, y, c: (ring[(place[z] + 1) % zs], y, c))
    back = pairs(lambda z, y, c: (ring[(place[z] - 1) % zs], y, c))
    across = pairs(lambda z, y, c: (z, (y + 1) % ys, c))
    twin = pairs(lambda z, y, c: (z, y, 1 - c))

    def permute(value, perm):
        return lax.ppermute(value, "wide", perm)

    lanes = {}

    def send(lane, value, perm, depth=0):
        got = lanes.setdefault(lane, [])
        if depth and len(got) >= depth:
            value = tie(value, got[-depth])
        got.append(permute(value, perm))
        return got[-1]

    chip = my_z * ys + col
    experts = jnp.stack([2 * chip + core, 2 * chip + 1 - core])
    if ys == 2:
        there = my_z * ys + 1 - col
        experts = jnp.concatenate([experts, jnp.stack([2 * there + core, 2 * there + 1 - core])])
    slots = 2 * cap

    def cut(value):
        step = width // STREAMS
        return [value[:, i * step : (i + 1) * step] for i in range(STREAMS)]

    half = width // STREAMS
    routes = jnp.concatenate([expert_ids, gate_codes // 32, gate_codes % 32], axis=1).astype(jnp.bfloat16)
    routes = jnp.pad(routes.T, ((0, rows - 3 * top), (0, 0)))
    blocks = {
        "tokens": [[jnp.concatenate([tokens[:, :half], routes], axis=1)] + cut(tokens)[1:]],
        "cot": [cut(cotangent)],
    }
    own, other = {"tokens": [], "cot": []}, {"tokens": [], "cot": []}
    tables = []

    def came(lane, index):
        got = lanes.get(lane, [])
        return got[index] if index < len(got) else None

    def onward(name, early=(), late=()):
        parts = blocks[name][-1]
        parts[0] = tie(parts[0], *early)
        parts[-1] = tie(parts[-1], *late)
        first = 1 if len(blocks[name]) == 1 else 0
        blocks[name].append([send(i, part, ahead, first) for i, part in enumerate(parts)])

    def choose(name, r, deps=()):
        deps = [dep for dep in deps if dep is not None]
        if name == "tokens":
            chosen, found = first_choice(experts, blocks[name][r], width, cap, top, deps)
            tables.append(found)
        else:
            chosen = next_choice(tables[r], blocks[name][r], width, cap, deps)
        own[name].append(chosen[0])
        if ys == 2:
            other[name].append(send("y", chosen[1], across))

    def homeward(results, r, depth=2):
        return send("y", results[zs + r], across, depth) if ys == 2 else None

    def combine(results, weighted, far=None):
        total, steps = [None] * STREAMS, []
        for r in reversed(range(zs)):
            pieces = [results[r]]
            if ys == 2:
                pieces.append(far if r == zs - 1 and far is not None else homeward(results, r))
            if r == 0:
                full = tokens
                for i in range(STREAMS):
                    full = back_sum(tables[0], weighted, pieces, total[i], i, STREAMS, full)
                return full, steps
            for i in range(STREAMS):
                value = back_sum(tables[r], weighted, pieces, total[i], i, STREAMS)
                total[i] = send(i, value, back, 1 if r == zs - 1 else 0)
            steps.append(list(total))

    def both(weight):
        return weight[0], permute(weight[0], twin)

    gate_mats, up_mats, down_mats = both(w_gate), both(w_up), both(w_down)
    twins = [gate_mats[1], up_mats[1], down_mats[1]]
    last = zs - 1
    choose("tokens", 0)
    choose("cot", 0)
    for r in range(1, zs):
        onward("tokens", [own["cot"][0] if r == 2 else own["tokens"][r - 2]] if r > 1 else [], [came("y", r - 2), *(twins if r == 2 else [])] if r > 1 else [])
        choose("tokens", r)
    for r in range(1, zs):
        if r == last:
            outs, saved = expert_forward(own["tokens"] + other["tokens"], gate_mats, up_mats, down_mats, cap)
        onward("cot", [own["tokens"][-1]] if r > 1 else [], [came("y", r + 1)] + ([outs[0]] if r == last else []))
        if r < last:
            choose("cot", r)
    far = homeward(outs, last)
    choose("cot", last, [outs[0]])
    moe_out, steps = combine(outs, True, far)
    deps = [came("y", 2 * zs + 1)] if ys == 2 else []
    grads = expert_backward(own["cot"] + other["cot"], saved, gate_mats, up_mats, down_mats, cap, deps + steps[0] + steps[1][:1])
    token_grad, _ = combine(grads, False)
    return (moe_out, token_grad)


def solution(mesh):
    return jax.shard_map(
        per_device,
        mesh=mesh,
        in_specs=(
            P(("group", "wide"), None),
            P(("group", "wide"), None),
            P(("group", "wide"), None),
            P(("group", "wide"), None),
            P("wide", None, None),
            P("wide", None, None),
            P("wide", None, None),
        ),
        out_specs=(P(("group", "wide"), None), P(("group", "wide"), None)),
        check_vma=False,
    )
```

```python
import jax
import jax.numpy as jnp
from jax import lax
from jax.experimental import pallas as pl
from jax.experimental.pallas import tpu as pltpu
from jax.sharding import PartitionSpec as P

contract_last = (((1,), (1,)), ((), ()))
contract_first = (((0,), (0,)), ((), ()))
STREAMS = 2


def layout(wide):
    if wide == 16:
        return 4, 2, (0, 1, 3, 2)
    return wide // 2, 1, tuple(range(wide // 2))


def tie(value, *others):
    others = [other for other in others if other is not None]
    if not others:
        return value
    return pl.pallas_call(
        lambda *refs: None,
        out_shape=jax.ShapeDtypeStruct(value.shape, value.dtype),
        in_specs=[pl.BlockSpec(memory_space=pl.ANY)] * (1 + len(others)),
        out_specs=pl.BlockSpec(memory_space=pl.ANY),
        input_output_aliases={0: 0},
        name="tie",
    )(value, *others)


def whole_spec(shape):
    return pl.BlockSpec(shape, lambda *_: (0,) * len(shape))


ANYWHERE = pl.BlockSpec(memory_space=pl.ANY)


def params(mib):
    return pltpu.CompilerParams(vmem_limit_bytes=mib * 2**20)


def pick_rows(parts, pick, weight, refs):
    start = 0
    for part in parts:
        stop = start + part.shape[1]
        rows = jnp.dot(pick, part, preferred_element_type=jnp.float32)
        if weight is not None:
            rows = weight * rows
        rows = rows.astype(jnp.bfloat16)
        at = 0
        for ref in refs:
            ref[:, start:stop] = rows[at : at + ref.shape[0]]
            at += ref.shape[0]
        start = stop


def first_choice(experts, parts, width, cap, top, deps):
    rows = parts[0].shape[0]
    half = width // len(parts)
    count = experts.shape[0]
    chips = count // 2

    def body(experts, *refs):
        parts = refs[: len(refs) - chips - 2 - len(deps)]
        outs = refs[len(refs) - chips - 2 : len(refs) - 2]
        pick_ref, gated_ref = refs[-2:]
        routes = parts[0][0:16, half : half + rows].astype(jnp.float32)
        line = [routes[j : j + 1] for j in range(3 * top)]
        codes = [line[top + j] * 32.0 + line[2 * top + j] for j in range(top)]
        total = sum(codes[1:], codes[0])
        share = [code / total for code in codes]
        ids = [value.astype(jnp.int32) for value in line[:top]]
        hits, gates = [], []
        for k in range(count):
            hit, gate = jnp.zeros((1, rows), jnp.float32), jnp.zeros((1, rows), jnp.float32)
            for j in range(top):
                same = ids[j] == experts[k]
                hit = jnp.where(same, 1.0, hit)
                gate = jnp.where(same, gate + share[j], gate)
            hits.append(hit)
            gates.append(gate)
        stacked = jnp.concatenate(hits + [jnp.zeros((8 - count, rows), jnp.float32)], axis=0)
        upto = lax.broadcasted_iota(jnp.int32, (rows, rows), 0) <= lax.broadcasted_iota(jnp.int32, (rows, rows), 1)
        upto = jnp.where(upto, 1.0, 0.0).astype(jnp.bfloat16)
        spot = jnp.dot(stacked.astype(jnp.bfloat16), upto, preferred_element_type=jnp.float32).astype(jnp.int32) - 1
        slot = lax.broadcasted_iota(jnp.int32, (cap, rows), 0)
        picks, gated = [], []
        for k in range(count):
            chosen = jnp.where(slot == spot[k : k + 1], jnp.broadcast_to(hits[k], (cap, rows)), 0.0)
            picks.append(chosen)
            gated.append(chosen * gates[k])
        pick = jnp.concatenate(picks, axis=0).astype(jnp.bfloat16)
        pick_ref[...] = pick
        gated_ref[...] = jnp.concatenate(gated, axis=0)
        pick_rows([parts[0][:, :half]] + [part[...] for part in parts[1:]], pick, None, outs)

    rows_of = jax.ShapeDtypeStruct((2 * cap, width), jnp.bfloat16)
    results = pl.pallas_call(
        body,
        grid=(1,),
        in_specs=[pl.BlockSpec(memory_space=pltpu.SMEM)]
        + [whole_spec(part.shape) for part in parts]
        + [ANYWHERE] * len(deps),
        out_specs=[whole_spec((2 * cap, width))] * chips + [whole_spec((count * cap, rows))] * 2,
        out_shape=[rows_of] * chips
        + [
            jax.ShapeDtypeStruct((count * cap, rows), jnp.bfloat16),
            jax.ShapeDtypeStruct((count * cap, rows), jnp.float32),
        ],
        compiler_params=params(24),
        name="first_choice",
    )(experts, *parts, *deps)
    return results[:chips], results[chips:]


def next_choice(tables, parts, width, cap, deps):
    pick, gated = tables
    chips = pick.shape[0] // (2 * cap)

    def body(pick, gated, *refs):
        parts = refs[: len(refs) - chips - len(deps)]
        weight = jnp.sum(gated[...], axis=1, keepdims=True)
        pick_rows([part[...] for part in parts], pick[...], weight, refs[len(refs) - chips :])

    return pl.pallas_call(
        body,
        grid=(1,),
        in_specs=[whole_spec(pick.shape), whole_spec(gated.shape)]
        + [whole_spec(part.shape) for part in parts]
        + [ANYWHERE] * len(deps),
        out_specs=[whole_spec((2 * cap, width))] * chips,
        out_shape=[jax.ShapeDtypeStruct((2 * cap, width), jnp.bfloat16)] * chips,
        compiler_params=params(24),
        name="next_choice",
    )(pick, gated, *parts, *deps)


def back_sum(tables, weighted, pieces, came, part, parts, full=None):
    pick, gated = tables
    rows = pick.shape[1]
    width = pieces[0].shape[1]
    step = width // parts
    final = full is not None

    def body(mix, *refs):
        out = refs[-1]
        at, total = 0, None
        if came is not None:
            total = refs[len(pieces)][...].astype(jnp.float32)
        for ref in refs[: len(pieces)]:
            share = mix[at : at + ref.shape[0]]
            at += ref.shape[0]
            if weighted:
                upper = share.astype(jnp.bfloat16)
                shares = [upper, (share - upper.astype(jnp.float32)).astype(jnp.bfloat16)]
            else:
                shares = [share]
            for value in shares:
                more = lax.dot_general(value, ref[...], contract_first, preferred_element_type=jnp.float32)
                total = more if total is None else total + more
        out[...] = total.astype(jnp.bfloat16)

    mix = gated if weighted else pick
    operands = [mix, *pieces]
    specs = [whole_spec(mix.shape)] + [pl.BlockSpec((piece.shape[0], step), lambda g: (0, part)) for piece in pieces]
    if came is not None:
        operands.append(came)
        specs.append(whole_spec((rows, step)))
    aliases = {}
    if final and part > 0:
        aliases = {len(operands): 0}
        operands.append(full)
        specs.append(ANYWHERE)
    return pl.pallas_call(
        body,
        grid=(1,),
        in_specs=specs,
        out_specs=pl.BlockSpec((rows, step), lambda g: (0, part if final else 0)),
        out_shape=jax.ShapeDtypeStruct((rows, width if final else step), jnp.bfloat16),
        input_output_aliases=aliases,
        compiler_params=params(24),
        name="back_sum",
    )(*operands)


TILE = 256
WIDE_TILE = 1024


def expert_call(body, pieces, extras, weights, scratch, more_outs, cap, width, hidden, name, deps):
    firsts, seconds = hidden // TILE, width // WIDE_TILE
    total = len(pieces) * cap

    def first(j):
        return jnp.minimum(j, firsts - 1)

    def second(j):
        return jnp.maximum(j - firsts, 0)

    def at(e, mine, index, last):
        return jnp.where(e == mine, index, 0 if mine else last)

    specs = [pl.BlockSpec(piece.shape, lambda e, j: (0, 0), pipeline_mode=pl.Buffered(1)) for piece in pieces]
    specs += [pl.BlockSpec((1, total, TILE), lambda e, j: (e, 0, first(j)))] * len(extras)
    operands = list(pieces) + list(extras)
    for pair, block, axis, stage in weights:
        for mine, weight in enumerate(pair):
            last = (firsts if stage == 0 else seconds) - 1

            def where(e, j, mine=mine, axis=axis, stage=stage, last=last):
                index = at(e, mine, first(j) if stage == 0 else second(j), last)
                return (index, 0) if axis == 0 else (0, index)

            specs.append(pl.BlockSpec(block, where))
            operands.append(weight)
    specs += [ANYWHERE] * len(deps)
    operands += deps
    out_specs = [pl.BlockSpec((cap, WIDE_TILE), lambda e, j: (e, second(j)))] * len(pieces)
    out_shape = [jax.ShapeDtypeStruct((2 * cap, width), jnp.bfloat16)] * len(pieces)
    out_specs += [pl.BlockSpec((1, total, TILE), lambda e, j: (e, 0, first(j)))] * len(more_outs)
    out_shape += more_outs
    size = 6 * total * width * hidden * 2
    return pl.pallas_call(
        body,
        grid=(2, firsts + seconds),
        in_specs=specs,
        out_specs=out_specs,
        out_shape=out_shape,
        scratch_shapes=scratch,
        compiler_params=params(56),
        cost_estimate=pl.CostEstimate(flops=size, bytes_accessed=12 * width * hidden + 8 * total * width, transcendentals=0),
        name=name,
    )(*operands)


def put_rows(pieces, rows, e, cap):
    for i, piece in enumerate(pieces):
        rows[i * cap : (i + 1) * cap] = piece[pl.ds(pl.multiple_of(e * cap, 16), cap)]


def take_rows(outs, value, cap):
    for i, out in enumerate(outs):
        out[...] = value[i * cap : (i + 1) * cap]


def expert_forward(pieces, gates, ups, downs, cap, deps=()):
    width, hidden = gates[0].shape
    total = len(pieces) * cap
    firsts = hidden // TILE

    def body(*refs):
        n = len(pieces)
        pieces_in, refs = refs[:n], refs[n:]
        (gate0, gate1, up0, up1, down0, down1), refs = refs[:6], refs[6 + len(deps) :]
        outs, (slope, active, rows, inner) = refs[:n], refs[n:]
        e, j = pl.program_id(0), pl.program_id(1)

        @pl.when(j == 0)
        def _():
            put_rows(pieces_in, rows, e, cap)

        def enter(gate, up):
            pre_gate = jnp.dot(rows[...], gate[...], preferred_element_type=jnp.float32)
            pre_up = jnp.dot(rows[...], up[...], preferred_element_type=jnp.float32)
            logistic = jax.nn.sigmoid(pre_gate)
            activated = pre_gate * logistic
            active[0] = activated
            slope[0] = pre_up * logistic * (1.0 + pre_gate * (1.0 - logistic))
            for k in range(firsts):

                @pl.when(j == k)
                def _():
                    inner[:, k * TILE : (k + 1) * TILE] = (activated * pre_up).astype(jnp.bfloat16)

        def leave(down):
            value = jnp.dot(inner[...], down[...], preferred_element_type=jnp.float32)
            take_rows(outs, value.astype(jnp.bfloat16), cap)

        for mine, (gate, up, down) in enumerate(((gate0, up0, down0), (gate1, up1, down1))):
            pl.when((e == mine) & (j < firsts))(lambda gate=gate, up=up: enter(gate, up))
            pl.when((e == mine) & (j >= firsts))(lambda down=down: leave(down))

    saved = jax.ShapeDtypeStruct((2, total, hidden), jnp.float32)
    weights = [
        (gates, (width, TILE), 1, 0),
        (ups, (width, TILE), 1, 0),
        (downs, (hidden, WIDE_TILE), 1, 1),
    ]
    scratch = [pltpu.VMEM((total, width), jnp.bfloat16), pltpu.VMEM((total, hidden), jnp.bfloat16)]
    results = expert_call(
        body, pieces, [], weights, scratch, [saved, saved], cap, width, hidden, "expert_forward", list(deps)
    )
    return list(results[:-2]), list(results[-2:])


def expert_backward(pieces, saved, gates, ups, downs, cap, deps=()):
    width, hidden = gates[0].shape
    total = len(pieces) * cap
    firsts = hidden // TILE

    def body(*refs):
        n = len(pieces)
        pieces_in, refs = refs[:n], refs[n:]
        (slope, active), refs = refs[:2], refs[2:]
        (down0, down1, gate0, gate1, up0, up1), refs = refs[:6], refs[6 + len(deps) :]
        outs, (rows, gate_grad, up_grad) = refs[:n], refs[n:]
        e, j = pl.program_id(0), pl.program_id(1)

        @pl.when(j == 0)
        def _():
            put_rows(pieces_in, rows, e, cap)

        def enter(down):
            hidden_grad = lax.dot_general(rows[...], down[...], contract_last, preferred_element_type=jnp.float32)
            for k in range(firsts):

                @pl.when(j == k)
                def _():
                    gate_grad[:, k * TILE : (k + 1) * TILE] = (hidden_grad * slope[0]).astype(jnp.bfloat16)
                    up_grad[:, k * TILE : (k + 1) * TILE] = (hidden_grad * active[0]).astype(jnp.bfloat16)

        def leave(gate, up):
            value = lax.dot_general(gate_grad[...], gate[...], contract_last, preferred_element_type=jnp.float32)
            value += lax.dot_general(up_grad[...], up[...], contract_last, preferred_element_type=jnp.float32)
            take_rows(outs, value.astype(jnp.bfloat16), cap)

        for mine, (gate, up, down) in enumerate(((gate0, up0, down0), (gate1, up1, down1))):
            pl.when((e == mine) & (j < firsts))(lambda down=down: enter(down))
            pl.when((e == mine) & (j >= firsts))(lambda gate=gate, up=up: leave(gate, up))

    weights = [
        (downs, (TILE, width), 0, 0),
        (gates, (WIDE_TILE, hidden), 0, 1),
        (ups, (WIDE_TILE, hidden), 0, 1),
    ]
    scratch = [pltpu.VMEM((total, width), jnp.bfloat16)] + [pltpu.VMEM((total, hidden), jnp.bfloat16)] * 2
    return expert_call(
        body, pieces, list(saved), weights, scratch, [], cap, width, hidden, "expert_backward", list(deps)
    )


def per_device(tokens, cotangent, expert_ids, gate_codes, w_gate, w_up, w_down):
    wide = lax.axis_size("wide")
    rows, width = tokens.shape
    top = expert_ids.shape[1]
    cap = -(-3 * rows * top // (2 * wide) // 16) * 16
    zs, ys, ring = layout(wide)
    me = lax.axis_index("wide")
    core, col, my_z = me % 2, (me // 2) % ys, me // (2 * ys)

    def pairs(move):
        out = []
        for z in range(zs):
            for y in range(ys):
                for c in range(2):
                    tz, ty, tc = move(z, y, c)
                    out.append(((z * ys + y) * 2 + c, (tz * ys + ty) * 2 + tc))
        return out

    place = {z: i for i, z in enumerate(ring)}
    ahead = pairs(lambda z, y, c: (ring[(place[z] + 1) % zs], y, c))
    back = pairs(lambda z, y, c: (ring[(place[z] - 1) % zs], y, c))
    across = pairs(lambda z, y, c: (z, (y + 1) % ys, c))
    twin = pairs(lambda z, y, c: (z, y, 1 - c))

    def permute(value, perm):
        return lax.ppermute(value, "wide", perm)

    lanes = {}

    def send(lane, value, perm, depth=0):
        got = lanes.setdefault(lane, [])
        if depth and len(got) >= depth:
            value = tie(value, got[-depth])
        got.append(permute(value, perm))
        return got[-1]

    chip = my_z * ys + col
    experts = jnp.stack([2 * chip + core, 2 * chip + 1 - core])
    if ys == 2:
        there = my_z * ys + 1 - col
        experts = jnp.concatenate([experts, jnp.stack([2 * there + core, 2 * there + 1 - core])])
    slots = 2 * cap

    def cut(value):
        step = width // STREAMS
        return [value[:, i * step : (i + 1) * step] for i in range(STREAMS)]

    half = width // STREAMS
    routes = jnp.concatenate([expert_ids, gate_codes // 32, gate_codes % 32], axis=1).astype(jnp.bfloat16)
    routes = jnp.pad(routes.T, ((0, rows - 3 * top), (0, 0)))
    blocks = {
        "tokens": [[jnp.concatenate([tokens[:, :half], routes], axis=1)] + cut(tokens)[1:]],
        "cot": [cut(cotangent)],
    }
    own, other = {"tokens": [], "cot": []}, {"tokens": [], "cot": []}
    tables = []

    def came(lane, index):
        got = lanes.get(lane, [])
        return got[index] if index < len(got) else None

    def onward(name, early=(), late=()):
        parts = blocks[name][-1]
        parts[0] = tie(parts[0], *early)
        parts[-1] = tie(parts[-1], *late)
        first = 1 if len(blocks[name]) == 1 else 0
        blocks[name].append([send(i, part, ahead, first) for i, part in enumerate(parts)])

    def choose(name, r, deps=()):
        deps = [dep for dep in deps if dep is not None]
        if name == "tokens":
            chosen, found = first_choice(experts, blocks[name][r], width, cap, top, deps)
            tables.append(found)
        else:
            chosen = next_choice(tables[r], blocks[name][r], width, cap, deps)
        own[name].append(chosen[0])
        if ys == 2:
            other[name].append(send("y", chosen[1], across))

    def homeward(results, r, depth=2):
        return send("y", results[zs + r], across, depth) if ys == 2 else None

    def combine(results, weighted, far=None):
        total, steps = [None] * STREAMS, []
        for r in reversed(range(zs)):
            pieces = [results[r]]
            if ys == 2:
                pieces.append(far if r == zs - 1 and far is not None else homeward(results, r))
            if r == 0:
                full = tokens
                for i in range(STREAMS):
                    full = back_sum(tables[0], weighted, pieces, total[i], i, STREAMS, full)
                return full, steps
            for i in range(STREAMS):
                value = back_sum(tables[r], weighted, pieces, total[i], i, STREAMS)
                total[i] = send(i, value, back, 1 if r == zs - 1 else 0)
            steps.append(list(total))

    def both(weight):
        return weight[0], permute(weight[0], twin)

    gate_mats, up_mats, down_mats = both(w_gate), both(w_up), both(w_down)
    twins = [gate_mats[1], up_mats[1], down_mats[1]]
    last = zs - 1
    choose("tokens", 0)
    choose("cot", 0)
    for r in range(1, zs):
        onward("tokens", [own["cot"][0] if r == 2 else own["tokens"][r - 2]] if r > 1 else [], [came("y", r - 2), *(twins if r == 2 else [])] if r > 1 else [])
        choose("tokens", r)
    for r in range(1, zs):
        if r == last:
            outs, saved = expert_forward(own["tokens"] + other["tokens"], gate_mats, up_mats, down_mats, cap)
        onward("cot", [own["tokens"][-1]] if r > 1 else [], [came("y", r + 1)] + ([outs[0]] if r == last else []))
        if r < last:
            choose("cot", r)
    far = homeward(outs, last)
    choose("cot", last, [outs[0]])
    moe_out, steps = combine(outs, True, far)
    deps = [came("y", 2 * zs + 1)] if ys == 2 else []
    grads = expert_backward(own["cot"] + other["cot"], saved, gate_mats, up_mats, down_mats, cap, deps + steps[0] + steps[1])
    token_grad, _ = combine(grads, False)
    return (moe_out, token_grad)


def solution(mesh):
    return jax.shard_map(
        per_device,
        mesh=mesh,
        in_specs=(
            P(("group", "wide"), None),
            P(("group", "wide"), None),
            P(("group", "wide"), None),
            P(("group", "wide"), None),
            P("wide", None, None),
            P("wide", None, None),
            P("wide", None, None),
        ),
        out_specs=(P(("group", "wide"), None), P(("group", "wide"), None)),
        check_vma=False,
    )
```
